32 devices in a mesh: dp: 16 (over z, x, core), rep: 2 (over y).
Axes of the slice: x: 2, y: 2, z: 4, core: 2. Of those that a mesh axis runs over, the one named last changes fastest.
Arguments:
- tokens: bfloat16 [49152, 768], P(('dp', 'rep')), may hold values from -12 to 12
- cotangent: bfloat16 [49152, 768], P(('dp', 'rep')), may hold values from -6 to 6
- lengths: int32 [96, 3], P(('dp', 'rep')), may hold values from 1 to 256, 512 in all within a row
- qkv_weight: float32 [768, 2304], P('dp'), may hold values from -0.21875 to 0.21875
- attn_out_weight: float32 [768, 768], P('dp'), may hold values from -1.75 to 1.75
- mlp_in_weight: float32 [768, 2304], P('dp'), may hold values from -0.21875 to 0.21875
- mlp_out_weight: float32 [1152, 768], P('dp'), may hold values from -0.1875 to 0.1875
- norm_gains: float32 [768, 2], P('dp'), may hold values from 0.5 to 1.5
- qkv_first: float32 [768, 2304], P('dp'), may hold values from -160 to 160
- qkv_second: float32 [768, 2304], P('dp'), may hold values from 1003.094 to 4012.4253
- attn_first: float32 [768, 768], P('dp'), may hold values from -20 to 20
- attn_second: float32 [768, 768], P('dp'), may hold values from 15.67359 to 62.693375
- mlp_in_first: float32 [768, 2304], P('dp'), may hold values from -80 to 80
- mlp_in_second: float32 [768, 2304], P('dp'), may hold values from 334.3663 to 1337.4751
- mlp_out_first: float32 [1152, 768], P('dp'), may hold values from -112 to 112
- mlp_out_second: float32 [1152, 768], P('dp'), may hold values from 501.547 to 2006.188
- gains_first: float32 [768, 2], P('dp'), may hold values from -160 to 160
- gains_second: float32 [768, 2], P('dp'), may hold values from 1003.094 to 4012.4253
Outputs:
- activations: bfloat16 [49152, 768], P(('dp', 'rep'))
- input_grad: float32 [49152, 768], P(('dp', 'rep'))
- qkv_new: float32 [768, 2304], P('dp')
- qkv_first_new: float32 [768, 2304], P('dp')
- qkv_second_new: float32 [768, 2304], P('dp')
- attn_out_new: float32 [768, 768], P('dp')
- attn_first_new: float32 [768, 768], P('dp')
- attn_second_new: float32 [768, 768], P('dp')
- mlp_in_new: float32 [768, 2304], P('dp')
- mlp_in_first_new: float32 [768, 2304], P('dp')
- mlp_in_second_new: float32 [768, 2304], P('dp')
- mlp_out_new: float32 [1152, 768], P('dp')
- mlp_out_first_new: float32 [1152, 768], P('dp')
- mlp_out_second_new: float32 [1152, 768], P('dp')
- gains_new: float32 [768, 2], P('dp')
- gains_first_new: float32 [768, 2], P('dp')
- gains_second_new: float32 [768, 2], P('dp')
The draws below stay inside these ranges and needn't reach their ends.
Inputs may be any that keep to these rules, and one draw needn't show every extreme that they name: Row m holds in order the lengths of the 3 sequences packed into micro-batch m; every row sums to 512.
All inputs are finite; a program needn't handle non-finite values.
Results may differ from the reference program's by a relative error of at most 0.014.
The reference program's roundings to bfloat16 on the way count: a program that leaves them out, or rounds other values in their place, can miss the bound.
Values may be sent and summed in bfloat16 or wider, within the bound.
A program may use at most 256 MiB of HBM per device.

```python
import math
import jax
import jax.numpy as jnp
import numpy as np
from jax import lax

D = 768
HEADS = 12
HEAD_DIM = 64
FF = 1152
TOK_MB = 512
SEQS = 3
STEP = 10
MBS_ALL = 96
ROWS_ALL = 49152


def with_spikes(values, stream_key, source, target, blocks, factor):
    owner, partner = [(jnp.arange(values.shape[position]) // (values.shape[position] // blocks)).reshape([-1 if axis == position else 1 for axis in range(values.ndim)]) for position in (source, target)]
    chosen = jax.random.permutation(stream_key, blocks)[partner]
    strong = (owner == chosen) | (owner == (partner + blocks // 2) % blocks)
    return jnp.where(strong, factor * values, values)


def levels(own_key, shape, pieces, low, largest):
    level = 1.0
    for axis_at, shards_of in pieces:
        heights = jax.random.uniform(jax.random.fold_in(jax.random.fold_in(own_key, 6), axis_at), (shards_of,), jnp.float32, low / len(pieces), largest / len(pieces))
        level = level * jnp.repeat(jnp.exp(heights), shape[axis_at] // shards_of).reshape((-1,) + (1,) * (len(shape) - 1 - axis_at))
    return level


def length_profile(amount, total, bound, lean):
    weights = [(1 << 20) // math.isqrt(rank ** lean) + 1 for rank in range(2, amount + 1)]
    rest, holding = total - bound - (amount - 1), [1] * (amount - 1)
    while rest > 0:
        candidates = [i for i in range(amount - 1) if holding[i] < bound]
        mass, left = sum([weights[i] for i in candidates]), rest
        for i in candidates:
            more = min(bound - holding[i], max(1, left * weights[i] // mass), rest)
            holding[i] = holding[i] + more
            rest = rest - more
    return np.array([bound] + holding)


def ragged(key, count, total, bound, slope):
    if count == 2:
        one = jax.random.randint(key, (), max(1, total - bound), min(bound, total - 1) + 1)
        return jnp.stack([one, total - one])
    sizes = jnp.asarray(length_profile(count, total, bound, slope), jnp.int32)
    pairs = (count - 1) // 2
    donor, sink = sizes[1:1 + 2 * pairs:2], sizes[2:2 + 2 * pairs:2]
    slack = jnp.minimum(donor - 1, bound - sink)
    passed = jax.random.randint(jax.random.fold_in(key, 1), (pairs,), 0, 1 << 20) % (slack + 1)
    sizes = sizes.at[1:1 + 2 * pairs:2].set(donor - passed).at[2:2 + 2 * pairs:2].set(sink + passed)
    return sizes[jax.random.permutation(jax.random.fold_in(key, 2), count)]


def bell_draw(rng, shape, deviation, most, pieces=(), kind=jnp.bfloat16):
    level = levels(rng, shape, pieces, -0.22, 0.18) if pieces else 1.0
    result = jax.random.normal(rng, shape, jnp.float32) * deviation * level
    return jnp.minimum(jnp.maximum(result, -most), most).astype(kind)


def heavy_noise(own_key, dims, scale, bound, shards, heavy, kind=jnp.bfloat16):
    drawn = scale * jax.random.normal(own_key, dims, jnp.float32)
    if shards:
        drawn = drawn * levels(own_key, dims, shards, -0.22, 0.18)
    return jnp.clip(with_spikes(drawn, jax.random.fold_in(own_key, 3), *heavy), -bound, bound).astype(kind)


def setup_inputs(seed: int = 0) -> dict:
    key_of = jax.random.split(jax.random.key(seed), 19)
    tokens = heavy_noise(key_of[0], (ROWS_ALL, D), 1.0, 12.0, ((0, 32),), (0, 1, 32, 2.75))
    cotangent = bell_draw(key_of[1], (ROWS_ALL, D), 1.0, 6.0, ((0, 32),))
    lengths = jax.vmap(lambda own: ragged(own, SEQS, TOK_MB, TOK_MB // 2, 2))(jax.random.split(key_of[2], MBS_ALL)).reshape((MBS_ALL, SEQS)).astype(jnp.int32)
    qkv_weight = bell_draw(key_of[3], (D, 3 * D), D ** -0.5, 0.21875, ((0, 16),), jnp.float32)
    attn_out_weight = bell_draw(key_of[4], (D, D), (D // 64) ** -0.5, 1.75, ((0, 16),), jnp.float32)
    mlp_in_weight = bell_draw(key_of[5], (D, 2 * FF), D ** -0.5, 0.21875, ((0, 16),), jnp.float32)
    mlp_out_weight = bell_draw(key_of[6], (FF, D), FF ** -0.5, 0.1875, ((0, 16),), jnp.float32)
    norm_gains = jnp.clip(1.0 + 0.1 * jax.random.normal(key_of[7], (D, 2), jnp.float32), 0.5, 1.5)
    qkv_first = bell_draw(key_of[8], (D, 3 * D), (ROWS_ALL ** 0.5 * 0.1111), 160.0, ((0, 16),), jnp.float32)
    qkv_second = jnp.clip(jnp.exp(math.log(4012.4253) - 1.3863067 * jax.random.uniform(key_of[9], (D, 3 * D), jnp.float32) ** levels(key_of[9], (D, 3 * D), ((0, 16),), -0.2, 0.2)), 1003.094, 4012.4253)
    attn_first = bell_draw(key_of[10], (D, D), (ROWS_ALL ** 0.5 * 0.013889), 20.0, ((0, 16),), jnp.float32)
    attn_second = jnp.clip(jnp.exp(math.log(62.693375) - 1.38627866 * jax.random.uniform(key_of[11], (D, D), jnp.float32) ** levels(key_of[11], (D, D), ((0, 16),), -0.2, 0.2)), 15.67359, 62.693375)
    mlp_in_first = bell_draw(key_of[12], (D, 2 * FF), (ROWS_ALL ** 0.5 * 0.06415), 80.0, ((0, 16),), jnp.float32)
    mlp_in_second = jnp.clip(jnp.exp(math.log(1337.4751) - 1.3863018 * jax.random.uniform(key_of[13], (D, 2 * FF), jnp.float32) ** levels(key_of[13], (D, 2 * FF), ((0, 16),), -0.2, 0.2)), 334.3663, 1337.4751)
    mlp_out_first = bell_draw(key_of[14], (FF, D), (ROWS_ALL ** 0.5 * 0.078567), 112.0, ((0, 16),), jnp.float32)
    mlp_out_second = jnp.clip(jnp.exp(math.log(2006.188) - 1.3862944 * jax.random.uniform(key_of[15], (FF, D), jnp.float32) ** levels(key_of[15], (FF, D), ((0, 16),), -0.2, 0.2)), 501.547, 2006.188)
    gains_first = bell_draw(key_of[16], (D, 2), (ROWS_ALL ** 0.5 * 0.1111), 160.0, ((0, 16),), jnp.float32)
    gains_second = jnp.clip(jnp.exp(math.log(4012.4253) - 1.3863067 * jax.random.uniform(key_of[17], (D, 2), jnp.float32) ** levels(key_of[17], (D, 2), ((0, 16),), -0.2, 0.2)), 1003.094, 4012.4253)
    return dict(tokens=tokens, cotangent=cotangent, lengths=lengths, qkv_weight=qkv_weight, attn_out_weight=attn_out_weight, mlp_in_weight=mlp_in_weight, mlp_out_weight=mlp_out_weight, norm_gains=norm_gains, qkv_first=qkv_first, qkv_second=qkv_second, attn_first=attn_first, attn_second=attn_second, mlp_in_first=mlp_in_first, mlp_in_second=mlp_in_second, mlp_out_first=mlp_out_first, mlp_out_second=mlp_out_second, gains_first=gains_first, gains_second=gains_second)


@jax.custom_vjp
def low(v):
    return lax.optimization_barrier(v.astype(jnp.bfloat16)).astype(jnp.float32)

@jax.custom_vjp
def low_back(v):
    return v

def low_keep(v):
    return (low(v), None)

def low_pass(kept, grad):
    return (grad,)

def back_keep(v):
    return (v, None)

def back_low(kept, grad):
    return (low(grad),)
low.defvjp(low_keep, low_pass)
low_back.defvjp(back_keep, back_low)
beta_one = 0.9
beta_two = 0.98
adam_eps = 1e-06
decay_rate = 1e-05

def normalize(values):
    centred = values - lax.optimization_barrier(jnp.mean(values, -1, keepdims=True))
    return centred * lax.rsqrt(lax.optimization_barrier(jnp.mean(centred * centred, -1, keepdims=True)) + 1e-05)

def rotate_half(values):
    half_dim = values.shape[-1] // 2
    return jnp.concatenate([-values[..., half_dim:], values[..., :half_dim]], -1)

def rope_tables(positions):
    freq_idx = jnp.arange(HEAD_DIM // 2).astype(jnp.float32)
    inv_freq = jnp.exp(freq_idx * (-2.0 * math.log(160000.0) / HEAD_DIM))
    angles = positions.astype(jnp.float32)[:, None] * inv_freq[None, :]
    angles = jnp.concatenate([angles, angles], -1)[:, None, :]
    return (jnp.cos(angles), jnp.sin(angles))

def segments(seq_lens):
    ends = jnp.cumsum(seq_lens).astype(jnp.int32)
    row_idx = jnp.arange(TOK_MB).astype(jnp.int32)
    seg_ids = lax.optimization_barrier(jnp.sum((row_idx[:, None] >= ends[None, :]).astype(jnp.int32), 1))
    starts = ends - seq_lens.astype(jnp.int32)
    pick = seg_ids[:, None] == jnp.arange(SEQS).astype(jnp.int32)[None, :]
    positions = row_idx - lax.optimization_barrier(jnp.sum(jnp.where(pick, starts[None, :], 0), 1)).astype(jnp.int32)
    return (seg_ids, positions)

def matmul(left, right):
    return jnp.dot(left, right, preferred_element_type=jnp.float32, precision=lax.Precision.HIGHEST)

def layer_block(x_rows, seg_ids, positions, w_qkv, w_attn, w_in, w_out, gains):
    row_count = x_rows.shape[0]
    h_one = low(normalize(x_rows) * gains[:, 0])
    qkv_all = low_back(matmul(h_one, w_qkv))
    q_part = qkv_all[:, :D].reshape(row_count, HEADS, HEAD_DIM)
    k_part = qkv_all[:, D:2 * D].reshape(row_count, HEADS, HEAD_DIM)
    v_part = qkv_all[:, 2 * D:].reshape(row_count, HEADS, HEAD_DIM)
    cos_tab, sin_tab = rope_tables(positions)
    q_rot = low(q_part * cos_tab + rotate_half(q_part) * sin_tab)
    k_rot = low(k_part * cos_tab + rotate_half(k_part) * sin_tab)
    v_low = low(v_part)
    scores = jnp.einsum('qhd,khd->hqk', q_rot, k_rot, precision=lax.Precision.HIGHEST) * 0.125
    scores = low_back(scores)
    same_seg = (seg_ids[:, None] == seg_ids[None, :])[None]
    probs = jax.nn.softmax(jnp.where(same_seg, scores, -1e+30), axis=-1)
    context = jnp.einsum('hqk,khd->qhd', low(probs), v_low, precision=lax.Precision.HIGHEST)
    context = low(low_back(context.reshape(row_count, D)))
    middle = x_rows + low_back(matmul(context, w_attn))
    h_two = low(normalize(middle) * gains[:, 1])
    gate_up = low_back(matmul(h_two, w_in))
    act_in = gate_up[:, :FF]
    gate_in = gate_up[:, FF:]
    hidden = low(jax.nn.gelu(act_in, approximate=False) * gate_in)
    return middle + low_back(matmul(hidden, w_out))

def adam_update(weight, first, second, grad, rate):
    first_new = beta_one * first + (1.0 - beta_one) * grad
    second_new = beta_two * second + (1.0 - beta_two) * grad * grad
    corr_one = 1.0 - beta_one ** STEP
    corr_two = 1.0 - beta_two ** STEP
    direction = first_new / corr_one / (jnp.sqrt(second_new / corr_two) + adam_eps)
    return (weight - rate * (direction + decay_rate * weight), first_new, second_new)

def reference(tokens, cotangent, lengths, qkv_weight, attn_out_weight, mlp_in_weight, mlp_out_weight, norm_gains, qkv_first, qkv_second, attn_first, attn_second, mlp_in_first, mlp_in_second, mlp_out_first, mlp_out_second, gains_first, gains_second):
    micro_total = lengths.shape[0]
    seg_all, pos_all = jax.vmap(segments)(lengths)
    x_all = tokens.astype(jnp.float32).reshape(micro_total, TOK_MB, D)

    def forward(x_in, w_qkv, w_attn, w_in, w_out, gains):
        low_qkv = low(w_qkv)
        low_attn = low(w_attn)
        low_in = low(w_in)
        low_out = low(w_out)
        low_gains = low(gains)

        def one_step(carry, items):
            return (carry, layer_block(items[0], items[1], items[2], low_qkv, low_attn, low_in, low_out, low_gains))
        _, results = lax.scan(jax.checkpoint(one_step), jnp.zeros((), jnp.float32), (x_in, seg_all, pos_all))
        return results
    outputs, pull = jax.vjp(forward, x_all, qkv_weight, attn_out_weight, mlp_in_weight, mlp_out_weight, norm_gains)
    grads = pull(cotangent.astype(jnp.float32).reshape(micro_total, TOK_MB, D))
    activations = outputs.reshape(tokens.shape).astype(jnp.bfloat16)
    input_grad = grads[0].reshape(tokens.shape)
    qkv_res = adam_update(qkv_weight, qkv_first, qkv_second, grads[1], 0.03)
    attn_res = adam_update(attn_out_weight, attn_first, attn_second, grads[2], 0.3)
    in_res = adam_update(mlp_in_weight, mlp_in_first, mlp_in_second, grads[3], 0.03)
    out_res = adam_update(mlp_out_weight, mlp_out_first, mlp_out_second, grads[4], 0.03)
    gain_res = adam_update(norm_gains, gains_first, gains_second, grads[5], 0.5)
    return (activations, input_grad, qkv_res[0], qkv_res[1], qkv_res[2], attn_res[0], attn_res[1], attn_res[2], in_res[0], in_res[1], in_res[2], out_res[0], out_res[1], out_res[2], gain_res[0], gain_res[1], gain_res[2])
```

```python
import functools
import math

import jax
import jax.numpy as jnp
from jax import lax
from jax.experimental import pallas as pl
from jax.experimental.pallas import tpu as pltpu
from jax.sharding import PartitionSpec as P

HEADS = 12
HEAD_DIM = 64
STEP = 10
PAIR = 2 * HEAD_DIM
PAIRS = HEADS // 2

beta_one = 0.9
beta_two = 0.98
adam_eps = 1e-06
decay_rate = 1e-05
inv_root_two = 0.7071067811865476
inv_root_tau = 0.3989422804014327


def normalize(values):
    centred = values - jnp.mean(values, -1, keepdims=True)
    inv_std = lax.rsqrt(jnp.mean(centred * centred, -1, keepdims=True) + 1e-05)
    return (centred * inv_std, inv_std)


def norm_back(grad_out, x_hat, inv_std, gain_col):
    scaled = grad_out * gain_col
    return inv_std * (
        scaled
        - jnp.mean(scaled, -1, keepdims=True)
        - x_hat * jnp.mean(scaled * x_hat, -1, keepdims=True)
    )


def rope_tables(positions):
    freq_idx = jnp.arange(HEAD_DIM // 2).astype(jnp.float32)
    inv_freq = jnp.exp(freq_idx * (-2.0 * math.log(160000.0) / HEAD_DIM))
    angles = positions.astype(jnp.float32)[:, None] * inv_freq[None, :]
    cos, sin = jnp.cos(angles), jnp.sin(angles)
    return (
        jnp.concatenate([cos, cos, cos, cos], -1),
        jnp.concatenate([-sin, sin, -sin, sin], -1),
    )


def segments(lengths, row_count):
    ends = jnp.cumsum(lengths, -1)
    row_idx = jnp.arange(row_count)
    seg_ids = jnp.sum((row_idx[None, :, None] >= ends[:, None, :]).astype(jnp.int32), -1)
    starts = ends - lengths
    pick = seg_ids[:, :, None] == jnp.arange(lengths.shape[1])[None, None, :]
    positions = row_idx[None, :] - jnp.sum(jnp.where(pick, starts[:, None, :], 0), -1)
    return (seg_ids, positions)


def contract_rows(left, right):
    return lax.dot_general(
        left, right, (((0,), (0,)), ((), ())), preferred_element_type=jnp.float32
    )


def contract_cols(left, right):
    return lax.dot_general(
        left, right, (((1,), (1,)), ((), ())), preferred_element_type=jnp.float32
    )


def lanes_of(shape):
    return lax.broadcasted_iota(jnp.int32, shape, 1)


def swap_halves(values):
    lane = lanes_of(values.shape)
    up = pltpu.roll(values, PAIR - HEAD_DIM // 2, 1)
    down = pltpu.roll(values, HEAD_DIM // 2, 1)
    return jnp.where(lane % HEAD_DIM < HEAD_DIM // 2, up, down)


def mask_lanes(seg_col, lane):
    own = (lane % HEAD_DIM) == seg_col
    key_side = jnp.where(own, 1.0, 0.0).astype(jnp.bfloat16)
    few = lane % HEAD_DIM < 8
    query_side = jnp.where(few & jnp.logical_not(own), -1e30, 0.0).astype(jnp.bfloat16)
    return (query_side, key_side)


def attn_fwd_kernel(q_ref, k_ref, v_ref, cos_ref, sin_ref, seg_ref, rot_ref, ctx_ref):
    pair = pl.program_id(1)
    width = ctx_ref.shape[1] * PAIRS
    cos, sin = cos_ref[...], sin_ref[...]
    q_raw, k_raw = q_ref[...], k_ref[...]
    q_rot = ((q_raw * cos + swap_halves(q_raw) * sin) * 0.125).astype(jnp.bfloat16)
    k_rot = (k_raw * cos + swap_halves(k_raw) * sin).astype(jnp.bfloat16)
    v_low = v_ref[...].astype(jnp.bfloat16)
    at = pl.multiple_of(pair * PAIR, PAIR)
    rot_ref[:, pl.ds(at, PAIR)] = q_rot
    rot_ref[:, pl.ds(at + width, PAIR)] = k_rot
    rot_ref[:, pl.ds(at + 2 * width, PAIR)] = v_low
    lane = lanes_of(q_raw.shape)
    query_side, key_side = mask_lanes(seg_ref[...], lane)
    parts = []
    for head in range(2):
        own = (lane // HEAD_DIM) == head
        q_h = jnp.where(own, q_rot, query_side)
        k_h = jnp.where(own, k_rot, key_side)
        scores = contract_cols(q_h, k_h)
        expo = jnp.exp(scores - jnp.max(scores, -1, keepdims=True))
        total = jnp.sum(expo, -1, keepdims=True)
        probs = (expo * (1.0 / total)).astype(jnp.bfloat16)
        parts.append(jnp.dot(probs, v_low, preferred_element_type=jnp.float32))
    ctx_ref[...] = jnp.where(lane < HEAD_DIM, parts[0], parts[1]).astype(jnp.bfloat16)


def attn_bwd_kernel(q_ref, k_ref, v_ref, dctx_ref, cos_ref, sin_ref, seg_ref, out_ref):
    step = pl.program_id(1)
    width = out_ref.shape[1] // 3
    q_rot, k_rot, v_low, dctx = q_ref[...], k_ref[...], v_ref[...], dctx_ref[...]
    lane = lanes_of(q_rot.shape)
    query_side, key_side = mask_lanes(seg_ref[...], lane)
    k_turned = k_rot.astype(jnp.float32).T.astype(jnp.bfloat16)
    dq_parts, dk_parts, dv_parts = [], [], []
    for head in range(2):
        own = (lane // HEAD_DIM) == head
        q_h = jnp.where(own, q_rot, query_side)
        k_h = jnp.where(own, k_rot, key_side)
        v_h = jnp.where(own, v_low, jnp.zeros_like(v_low))
        scores = contract_cols(k_h, q_h)
        expo = jnp.exp(scores - jnp.max(scores, 0, keepdims=True))
        total = jnp.sum(expo, 0, keepdims=True)
        probs = expo * (1.0 / total)
        grad_probs = contract_cols(v_h, dctx)
        weighted = probs * grad_probs
        row_dots = jnp.sum(weighted, 0, keepdims=True)
        grad_scores = (weighted - probs * row_dots).astype(jnp.bfloat16)
        probs_low = probs.astype(jnp.bfloat16)
        dk_parts.append(jnp.dot(grad_scores, q_rot, preferred_element_type=jnp.float32))
        dv_parts.append(jnp.dot(probs_low, dctx, preferred_element_type=jnp.float32))
        dq_parts.append(
            jnp.dot(
                k_turned[head * HEAD_DIM : (head + 1) * HEAD_DIM],
                grad_scores,
                preferred_element_type=jnp.float32,
            )
        )
    cos, sin = cos_ref[...], sin_ref[...]
    dq = jnp.concatenate(dq_parts, 0).T * 0.125
    dk = jnp.where(lane < HEAD_DIM, dk_parts[0], dk_parts[1])
    dv = jnp.where(lane < HEAD_DIM, dv_parts[0], dv_parts[1])
    at = pl.multiple_of(step * PAIR, PAIR)
    out_ref[:, pl.ds(at, PAIR)] = (dq * cos - swap_halves(dq) * sin).astype(jnp.bfloat16)
    out_ref[:, pl.ds(at + width, PAIR)] = (dk * cos - swap_halves(dk) * sin).astype(jnp.bfloat16)
    out_ref[:, pl.ds(at + 2 * width, PAIR)] = dv.astype(jnp.bfloat16)


def attn_forward(qkv_all, cos_tab, sin_tab, seg_col, micro):
    rows = qkv_all.shape[0] // micro
    width = qkv_all.shape[1] // 3
    table = pl.BlockSpec((rows, PAIR), lambda m, p: (m, 0))
    return pl.pallas_call(
        attn_fwd_kernel,
        grid=(micro, PAIRS),
        in_specs=[
            pl.BlockSpec((rows, PAIR), lambda m, p: (m, p)),
            pl.BlockSpec((rows, PAIR), lambda m, p: (m, PAIRS + p)),
            pl.BlockSpec((rows, PAIR), lambda m, p: (m, 2 * PAIRS + p)),
            table,
            table,
            table,
        ],
        out_specs=[
            pl.BlockSpec((rows, 3 * width), lambda m, p: (m, 0)),
            pl.BlockSpec((rows, PAIR), lambda m, p: (m, p)),
        ],
        out_shape=[
            jax.ShapeDtypeStruct(qkv_all.shape, jnp.bfloat16),
            jax.ShapeDtypeStruct((qkv_all.shape[0], width), jnp.bfloat16),
        ],
        compiler_params=pltpu.CompilerParams(vmem_limit_bytes=40 * 1024 * 1024),
        cost_estimate=pl.CostEstimate(
            flops=micro * HEADS * 4 * rows * rows * PAIR,
            bytes_accessed=qkv_all.size * 7,
            transcendentals=micro * HEADS * rows * rows,
        ),
    )(qkv_all, qkv_all, qkv_all, cos_tab, sin_tab, seg_col)


def attn_backward(rot, dctx, cos_tab, sin_tab, seg_col, micro, first, count):
    rows = rot.shape[0] // micro
    table = pl.BlockSpec((rows, PAIR), lambda m, p: (m, 0))
    return pl.pallas_call(
        attn_bwd_kernel,
        grid=(micro, count),
        in_specs=[
            pl.BlockSpec((rows, PAIR), lambda m, p: (m, first + p)),
            pl.BlockSpec((rows, PAIR), lambda m, p: (m, PAIRS + first + p)),
            pl.BlockSpec((rows, PAIR), lambda m, p: (m, 2 * PAIRS + first + p)),
            pl.BlockSpec((rows, PAIR), lambda m, p: (m, first + p)),
            table,
            table,
            table,
        ],
        out_specs=pl.BlockSpec((rows, 3 * count * PAIR), lambda m, p: (m, 0)),
        out_shape=jax.ShapeDtypeStruct((rot.shape[0], 3 * count * PAIR), jnp.bfloat16),
        compiler_params=pltpu.CompilerParams(vmem_limit_bytes=40 * 1024 * 1024),
        cost_estimate=pl.CostEstimate(
            flops=micro * count * 20 * rows * rows * PAIR,
            bytes_accessed=rot.shape[0] * count * PAIR * 14,
            transcendentals=micro * count * 2 * rows * rows,
        ),
    )(rot, rot, rot, dctx, cos_tab, sin_tab, seg_col)


def adam_update(weight, first, second, grad, rate):
    first_new = beta_one * first + (1.0 - beta_one) * grad
    second_new = beta_two * second + (1.0 - beta_two) * grad * grad
    corr_one = 1.0 - beta_one**STEP
    corr_two = 1.0 - beta_two**STEP
    direction = first_new / corr_one / (jnp.sqrt(second_new / corr_two) + adam_eps)
    return (weight - rate * (direction + decay_rate * weight), first_new, second_new)


def local(
    rep_size,
    tokens,
    cotangent,
    lengths,
    qkv_weight,
    attn_out_weight,
    mlp_in_weight,
    mlp_out_weight,
    norm_gains,
    qkv_first,
    qkv_second,
    attn_first,
    attn_second,
    mlp_in_first,
    mlp_in_second,
    mlp_out_first,
    mlp_out_second,
    gains_first,
    gains_second,
):
    micro = lengths.shape[0]
    rows = tokens.shape[0] // micro
    width = tokens.shape[1]
    ff_width = mlp_in_weight.shape[1] // 2

    def gather(value):
        return lax.all_gather(value, "dp", axis=0, tiled=True)

    def reduce_owned(value):
        part = lax.psum_scatter(value, "dp", scatter_dimension=0, tiled=True)
        other = lax.ppermute(part, "rep", [(i, rep_size - 1 - i) for i in range(rep_size)])
        return part.astype(jnp.float32) + other.astype(jnp.float32)

    padded_gains = jnp.pad(norm_gains, ((0, 0), (0, 126)))
    packed = gather(jnp.concatenate([qkv_weight, padded_gains], 1).astype(jnp.bfloat16))
    w_attn = gather(attn_out_weight.astype(jnp.bfloat16))
    w_in = gather(mlp_in_weight.astype(jnp.bfloat16))
    w_out = gather(mlp_out_weight.astype(jnp.bfloat16))
    w_qkv = packed[:, : 3 * width]
    gain_one = packed[:, 3 * width].astype(jnp.float32)
    gain_two = packed[:, 3 * width + 1].astype(jnp.float32)

    seg_ids, positions = segments(lengths, rows)
    cos_tab, sin_tab = rope_tables(positions.reshape(-1))
    seg_col = jnp.broadcast_to(seg_ids.reshape(-1, 1), (micro * rows, PAIR))

    x_float = tokens.astype(jnp.float32)
    hat_one, inv_one = normalize(x_float)
    h_one = (hat_one * gain_one).astype(jnp.bfloat16)
    qkv_all = jnp.dot(h_one, w_qkv, preferred_element_type=jnp.float32)
    rot, context = attn_forward(qkv_all, cos_tab, sin_tab, seg_col, micro)
    middle = x_float + jnp.dot(context, w_attn, preferred_element_type=jnp.float32)
    hat_two, inv_two = normalize(middle)
    h_two = (hat_two * gain_two).astype(jnp.bfloat16)
    gate_up = jnp.dot(h_two, w_in, preferred_element_type=jnp.float32)
    act_in = gate_up[:, :ff_width]
    gate_in = gate_up[:, ff_width:]
    cdf_vals = 0.5 * (1.0 + lax.erf(act_in * inv_root_two))
    act_out = act_in * cdf_vals
    hidden = (act_out * gate_in).astype(jnp.bfloat16)

    grad_float = cotangent.astype(jnp.float32)
    grad_hidden = contract_cols(cotangent, w_out)
    grad_wo = contract_rows(hidden, cotangent).astype(jnp.bfloat16)
    sum_o = reduce_owned(grad_wo)
    activations = (middle + jnp.dot(hidden, w_out, preferred_element_type=jnp.float32)).astype(
        jnp.bfloat16
    )
    grad_act = (
        grad_hidden * gate_in * (cdf_vals + act_in * inv_root_tau * jnp.exp(-0.5 * act_in * act_in))
    )
    grad_gate = grad_hidden * act_out
    grad_gu = jnp.concatenate([grad_act, grad_gate], 1).astype(jnp.bfloat16)
    sum_i = reduce_owned(contract_rows(h_two, grad_gu).astype(jnp.bfloat16))
    grad_h_two = contract_cols(grad_gu, w_in)
    grad_mid = grad_float + norm_back(grad_h_two, hat_two, inv_two, gain_two)
    grad_g_two = jnp.sum(grad_h_two * hat_two, 0)
    grad_mid_low = grad_mid.astype(jnp.bfloat16)
    sum_a = reduce_owned(contract_rows(context, grad_mid_low).astype(jnp.bfloat16))
    grad_ctx = contract_cols(grad_mid_low, w_attn).astype(jnp.bfloat16)

    half = PAIRS // 2
    side = half * PAIR
    grads_qkv, sums_q = [], []
    grad_h_one = None
    for part in range(2):
        grad_qkv = attn_backward(
            rot, grad_ctx, cos_tab, sin_tab, seg_col, micro, part * half, half
        )
        w_part = jnp.concatenate(
            [
                w_qkv[:, n * width + part * side : n * width + (part + 1) * side]
                for n in range(3)
            ],
            1,
        )
        term = contract_cols(grad_qkv, w_part)
        grad_h_one = term if grad_h_one is None else grad_h_one + term
        grad_wq = contract_rows(h_one, grad_qkv).astype(jnp.bfloat16)
        if part == 0:
            sums_q.append(reduce_owned(grad_wq))
    grad_g_one = jnp.sum(grad_h_one * hat_one, 0)
    grad_gains = jnp.stack([grad_g_one, grad_g_two], 1).astype(jnp.bfloat16)
    tail = reduce_owned(
        jnp.concatenate([grad_wq, jnp.pad(grad_gains, ((0, 0), (0, 126)))], 1)
    )
    sums_q.append(tail[:, : 3 * side])
    sum_g = tail[:, 3 * side : 3 * side + 2]
    input_grad = grad_mid + norm_back(grad_h_one, hat_one, inv_one, gain_one)
    sum_q = jnp.concatenate(
        [sums_q[part][:, n * side : (n + 1) * side] for n in range(3) for part in range(2)], 1
    )

    qkv_res = adam_update(qkv_weight, qkv_first, qkv_second, sum_q, 0.03)
    attn_res = adam_update(attn_out_weight, attn_first, attn_second, sum_a, 0.3)
    in_res = adam_update(mlp_in_weight, mlp_in_first, mlp_in_second, sum_i, 0.03)
    out_res = adam_update(mlp_out_weight, mlp_out_first, mlp_out_second, sum_o, 0.03)
    gain_res = adam_update(norm_gains, gains_first, gains_second, sum_g, 0.5)
    return (activations, input_grad, *qkv_res, *attn_res, *in_res, *out_res, *gain_res)


def solution(mesh):
    rows_spec = P(("dp", "rep"), None)
    owned = P("dp", None)
    return jax.shard_map(
        functools.partial(local, mesh.shape["rep"]),
        mesh=mesh,
        in_specs=(rows_spec,) * 3 + (owned,) * 15,
        out_specs=(rows_spec,) * 2 + (owned,) * 15,
        check_vma=False,
    )
```

```python
import functools
import math

import jax
import jax.numpy as jnp
from jax import lax
from jax.experimental import pallas as pl
from jax.experimental.layout import Layout, with_layout_constraint
from jax.experimental.pallas import tpu as pltpu
from jax.sharding import PartitionSpec as P

HEADS = 12
HEAD_DIM = 64
STEP = 10
PAIR = 2 * HEAD_DIM
PAIRS = HEADS // 2

beta_one = 0.9
beta_two = 0.98
adam_eps = 1e-06
decay_rate = 1e-05
inv_root_two = 0.7071067811865476
inv_root_tau = 0.3989422804014327


def row_major(values):
    return with_layout_constraint(values, Layout(major_to_minor=(0, 1)))


def normalize(values):
    centred = values - jnp.mean(values, -1, keepdims=True)
    inv_std = lax.rsqrt(jnp.mean(centred * centred, -1, keepdims=True) + 1e-05)
    return (centred * inv_std, inv_std)


def norm_back(grad_out, x_hat, inv_std, gain_col):
    scaled = grad_out * gain_col
    return inv_std * (
        scaled
        - jnp.mean(scaled, -1, keepdims=True)
        - x_hat * jnp.mean(scaled * x_hat, -1, keepdims=True)
    )


def rope_tables(positions):
    freq_idx = jnp.arange(HEAD_DIM // 2).astype(jnp.float32)
    inv_freq = jnp.exp(freq_idx * (-2.0 * math.log(160000.0) / HEAD_DIM))
    angles = positions.astype(jnp.float32)[:, None] * inv_freq[None, :]
    cos, sin = jnp.cos(angles), jnp.sin(angles)
    return (
        jnp.concatenate([cos, cos, cos, cos], -1),
        jnp.concatenate([-sin, sin, -sin, sin], -1),
    )


def segments(lengths, row_count):
    ends = jnp.cumsum(lengths, -1)
    row_idx = jnp.arange(row_count)
    seg_ids = jnp.sum((row_idx[None, :, None] >= ends[:, None, :]).astype(jnp.int32), -1)
    starts = ends - lengths
    pick = seg_ids[:, :, None] == jnp.arange(lengths.shape[1])[None, None, :]
    positions = row_idx[None, :] - jnp.sum(jnp.where(pick, starts[:, None, :], 0), -1)
    return (seg_ids, positions)


def contract_rows(left, right):
    return lax.dot_general(
        left, right, (((0,), (0,)), ((), ())), preferred_element_type=jnp.float32
    )


def contract_cols(left, right):
    return lax.dot_general(
        left, right, (((1,), (1,)), ((), ())), preferred_element_type=jnp.float32
    )


def lanes_of(shape):
    return lax.broadcasted_iota(jnp.int32, shape, 1)


def swap_halves(values):
    lane = lanes_of(values.shape)
    up = pltpu.roll(values, PAIR - HEAD_DIM // 2, 1)
    down = pltpu.roll(values, HEAD_DIM // 2, 1)
    return jnp.where(lane % HEAD_DIM < HEAD_DIM // 2, up, down)


def mask_lanes(seg_col, lane):
    own = (lane % HEAD_DIM) == seg_col
    key_side = jnp.where(own, 1.0, 0.0).astype(jnp.bfloat16)
    few = lane % HEAD_DIM < 8
    query_side = jnp.where(few & jnp.logical_not(own), -1e30, 0.0).astype(jnp.bfloat16)
    return (query_side, key_side)


def attn_fwd_kernel(q_ref, k_ref, v_ref, cos_ref, sin_ref, seg_ref, rot_ref, ctx_ref):
    pair = pl.program_id(1)
    width = ctx_ref.shape[1] * PAIRS
    cos, sin = cos_ref[...], sin_ref[...]
    q_raw, k_raw = q_ref[...], k_ref[...]
    q_rot = ((q_raw * cos + swap_halves(q_raw) * sin) * 0.125).astype(jnp.bfloat16)
    k_rot = (k_raw * cos + swap_halves(k_raw) * sin).astype(jnp.bfloat16)
    v_low = v_ref[...].astype(jnp.bfloat16)
    at = pl.multiple_of(pair * PAIR, PAIR)
    rot_ref[:, pl.ds(at, PAIR)] = q_rot
    rot_ref[:, pl.ds(at + width, PAIR)] = k_rot
    rot_ref[:, pl.ds(at + 2 * width, PAIR)] = v_low
    lane = lanes_of(q_raw.shape)
    query_side, key_side = mask_lanes(seg_ref[...], lane)
    parts = []
    for head in range(2):
        own = (lane // HEAD_DIM) == head
        q_h = jnp.where(own, q_rot, query_side)
        k_h = jnp.where(own, k_rot, key_side)
        scores = contract_cols(q_h, k_h)
        expo = jnp.exp(scores - jnp.max(scores, -1, keepdims=True))
        total = jnp.sum(expo, -1, keepdims=True)
        probs = (expo * (1.0 / total)).astype(jnp.bfloat16)
        parts.append(jnp.dot(probs, v_low, preferred_element_type=jnp.float32))
    ctx_ref[...] = jnp.where(lane < HEAD_DIM, parts[0], parts[1]).astype(jnp.bfloat16)


def attn_bwd_kernel(q_ref, k_ref, v_ref, dctx_ref, cos_ref, sin_ref, seg_ref, out_ref):
    step = pl.program_id(1)
    width = out_ref.shape[1] // 3
    q_rot, k_rot, v_low, dctx = q_ref[...], k_ref[...], v_ref[...], dctx_ref[...]
    lane = lanes_of(q_rot.shape)
    query_side, key_side = mask_lanes(seg_ref[...], lane)
    k_turned = k_rot.astype(jnp.float32).T.astype(jnp.bfloat16)
    dq_parts, dk_parts, dv_parts = [], [], []
    for head in range(2):
        own = (lane // HEAD_DIM) == head
        q_h = jnp.where(own, q_rot, query_side)
        k_h = jnp.where(own, k_rot, key_side)
        v_h = jnp.where(own, v_low, jnp.zeros_like(v_low))
        scores = contract_cols(k_h, q_h)
        expo = jnp.exp(scores - jnp.max(scores, 0, keepdims=True))
        total = jnp.sum(expo, 0, keepdims=True)
        probs = expo * (1.0 / total)
        grad_probs = contract_cols(v_h, dctx)
        weighted = probs * grad_probs
        row_dots = jnp.sum(weighted, 0, keepdims=True)
        grad_scores = (weighted - probs * row_dots).astype(jnp.bfloat16)
        probs_low = probs.astype(jnp.bfloat16)
        dk_parts.append(jnp.dot(grad_scores, q_rot, preferred_element_type=jnp.float32))
        dv_parts.append(jnp.dot(probs_low, dctx, preferred_element_type=jnp.float32))
        dq_parts.append(
            jnp.dot(
                k_turned[head * HEAD_DIM : (head + 1) * HEAD_DIM],
                grad_scores,
                preferred_element_type=jnp.float32,
            )
        )
    cos, sin = cos_ref[...], sin_ref[...]
    dq = jnp.concatenate(dq_parts, 0).T * 0.125
    dk = jnp.where(lane < HEAD_DIM, dk_parts[0], dk_parts[1])
    dv = jnp.where(lane < HEAD_DIM, dv_parts[0], dv_parts[1])
    at = pl.multiple_of(step * PAIR, PAIR)
    out_ref[:, pl.ds(at, PAIR)] = (dq * cos - swap_halves(dq) * sin).astype(jnp.bfloat16)
    out_ref[:, pl.ds(at + width, PAIR)] = (dk * cos - swap_halves(dk) * sin).astype(jnp.bfloat16)
    out_ref[:, pl.ds(at + 2 * width, PAIR)] = dv.astype(jnp.bfloat16)


def attn_forward(qkv_all, cos_tab, sin_tab, seg_col, micro):
    rows = qkv_all.shape[0] // micro
    width = qkv_all.shape[1] // 3
    table = pl.BlockSpec((rows, PAIR), lambda m, p: (m, 0))
    return pl.pallas_call(
        attn_fwd_kernel,
        grid=(micro, PAIRS),
        in_specs=[
            pl.BlockSpec((rows, PAIR), lambda m, p: (m, p)),
            pl.BlockSpec((rows, PAIR), lambda m, p: (m, PAIRS + p)),
            pl.BlockSpec((rows, PAIR), lambda m, p: (m, 2 * PAIRS + p)),
            table,
            table,
            table,
        ],
        out_specs=[
            pl.BlockSpec((rows, 3 * width), lambda m, p: (m, 0)),
            pl.BlockSpec((rows, PAIR), lambda m, p: (m, p)),
        ],
        out_shape=[
            jax.ShapeDtypeStruct(qkv_all.shape, jnp.bfloat16),
            jax.ShapeDtypeStruct((qkv_all.shape[0], width), jnp.bfloat16),
        ],
        compiler_params=pltpu.CompilerParams(vmem_limit_bytes=40 * 1024 * 1024),
        cost_estimate=pl.CostEstimate(
            flops=micro * HEADS * 4 * rows * rows * PAIR,
            bytes_accessed=qkv_all.size * 7,
            transcendentals=micro * HEADS * rows * rows,
        ),
    )(qkv_all, qkv_all, qkv_all, cos_tab, sin_tab, seg_col)


def attn_backward(rot, dctx, cos_tab, sin_tab, seg_col, micro, first, count):
    rows = rot.shape[0] // micro
    table = pl.BlockSpec((rows, PAIR), lambda m, p: (m, 0))
    return pl.pallas_call(
        attn_bwd_kernel,
        grid=(micro, count),
        in_specs=[
            pl.BlockSpec((rows, PAIR), lambda m, p: (m, first + p)),
            pl.BlockSpec((rows, PAIR), lambda m, p: (m, PAIRS + first + p)),
            pl.BlockSpec((rows, PAIR), lambda m, p: (m, 2 * PAIRS + first + p)),
            pl.BlockSpec((rows, PAIR), lambda m, p: (m, first + p)),
            table,
            table,
            table,
        ],
        out_specs=pl.BlockSpec((rows, 3 * count * PAIR), lambda m, p: (m, 0)),
        out_shape=jax.ShapeDtypeStruct((rot.shape[0], 3 * count * PAIR), jnp.bfloat16),
        compiler_params=pltpu.CompilerParams(vmem_limit_bytes=40 * 1024 * 1024),
        cost_estimate=pl.CostEstimate(
            flops=micro * count * 20 * rows * rows * PAIR,
            bytes_accessed=rot.shape[0] * count * PAIR * 14,
            transcendentals=micro * count * 2 * rows * rows,
        ),
    )(rot, rot, rot, dctx, cos_tab, sin_tab, seg_col)


def adam_update(weight, first, second, grad, rate):
    first_new = beta_one * first + (1.0 - beta_one) * grad
    second_new = beta_two * second + (1.0 - beta_two) * grad * grad
    corr_one = 1.0 - beta_one**STEP
    corr_two = 1.0 - beta_two**STEP
    direction = first_new / corr_one / (jnp.sqrt(second_new / corr_two) + adam_eps)
    return (weight - rate * (direction + decay_rate * weight), first_new, second_new)


def local(
    rep_size,
    tokens,
    cotangent,
    lengths,
    qkv_weight,
    attn_out_weight,
    mlp_in_weight,
    mlp_out_weight,
    norm_gains,
    qkv_first,
    qkv_second,
    attn_first,
    attn_second,
    mlp_in_first,
    mlp_in_second,
    mlp_out_first,
    mlp_out_second,
    gains_first,
    gains_second,
):
    micro = lengths.shape[0]
    rows = tokens.shape[0] // micro
    width = tokens.shape[1]
    ff_width = mlp_in_weight.shape[1] // 2

    def gather(value):
        return lax.all_gather(value, "dp", axis=0, tiled=True)

    def scatter(value):
        return lax.psum_scatter(value, "dp", scatter_dimension=0, tiled=True)

    def both_replicas(part):
        other = lax.ppermute(part, "rep", [(i, rep_size - 1 - i) for i in range(rep_size)])
        return row_major(part.astype(jnp.float32) + other.astype(jnp.float32))

    owners = width // qkv_weight.shape[0]
    own = qkv_weight.shape[0]
    rest = mlp_out_weight.shape[0] - own
    fold = own // rest

    def fold_rows(value):
        blocks = value.reshape(-1, own + rest, width)
        head = blocks[:, :own].reshape(-1, width)
        tail = blocks[:, own:]
        piece = width // fold
        tail = jnp.concatenate([tail[:, :, n * piece : (n + 1) * piece] for n in range(fold)], 1)
        return head, tail.reshape(-1, piece)

    def unfold_rows(head, tail):
        piece = width // fold
        blocks = tail.reshape(-1, own, piece)
        tail = jnp.concatenate([blocks[:, n * rest : (n + 1) * rest] for n in range(fold)], 2)
        return jnp.concatenate([head.reshape(-1, own, width), tail], 1).reshape(-1, width)

    padded_gains = row_major(jnp.pad(norm_gains, ((0, 0), (0, 126))).astype(jnp.bfloat16))
    packed = gather(jnp.concatenate([qkv_weight.astype(jnp.bfloat16), padded_gains], 1))
    w_qkv = packed[:, : 3 * width]
    gain_one = packed[:, 3 * width].astype(jnp.float32)
    gain_two = packed[:, 3 * width + 1].astype(jnp.float32)
    others = gather(
        jnp.concatenate(
            [
                mlp_in_weight.astype(jnp.bfloat16),
                attn_out_weight.astype(jnp.bfloat16),
                *fold_rows(mlp_out_weight.astype(jnp.bfloat16)),
            ],
            1,
        )
    )
    at_a, at_o = 2 * ff_width, 2 * ff_width + width
    w_in = others[:, :at_a]
    w_attn = others[:, at_a:at_o]
    w_out = unfold_rows(others[:, at_o : at_o + width], others[:, at_o + width :])

    seg_ids, positions = segments(lengths, rows)
    cos_tab, sin_tab = rope_tables(positions.reshape(-1))
    seg_col = jnp.broadcast_to(seg_ids.reshape(-1, 1), (micro * rows, PAIR))

    x_float = tokens.astype(jnp.float32)
    hat_one, inv_one = normalize(x_float)
    h_one = (hat_one * gain_one).astype(jnp.bfloat16)
    qkv_all = jnp.dot(h_one, w_qkv, preferred_element_type=jnp.float32)
    rot, context = attn_forward(qkv_all, cos_tab, sin_tab, seg_col, micro)
    middle = row_major(x_float + jnp.dot(context, w_attn, preferred_element_type=jnp.float32))
    hat_two, inv_two = normalize(middle)
    h_two = (hat_two * gain_two).astype(jnp.bfloat16)
    gate_up = jnp.dot(h_two, w_in, preferred_element_type=jnp.float32)
    act_in = gate_up[:, :ff_width]
    gate_in = gate_up[:, ff_width:]
    cdf_vals = 0.5 * (1.0 + lax.erf(act_in * inv_root_two))
    act_out = act_in * cdf_vals
    hidden = (act_out * gate_in).astype(jnp.bfloat16)

    grad_float = cotangent.astype(jnp.float32)
    grad_hidden = contract_cols(cotangent, w_out)
    grad_wo = contract_rows(hidden, cotangent).astype(jnp.bfloat16)
    activations = (middle + jnp.dot(hidden, w_out, preferred_element_type=jnp.float32)).astype(
        jnp.bfloat16
    )
    grad_act = (
        grad_hidden * gate_in * (cdf_vals + act_in * inv_root_tau * jnp.exp(-0.5 * act_in * act_in))
    )
    grad_gate = grad_hidden * act_out
    grad_gu = jnp.concatenate([grad_act, grad_gate], 1).astype(jnp.bfloat16)
    grad_wi = contract_rows(h_two, grad_gu).astype(jnp.bfloat16)
    grad_h_two = row_major(contract_cols(grad_gu, w_in))
    grad_mid = grad_float + norm_back(grad_h_two, hat_two, inv_two, gain_two)
    grad_g_two = jnp.sum(grad_h_two * hat_two, 0)
    grad_mid_low = grad_mid.astype(jnp.bfloat16)
    grad_wa = contract_rows(context, grad_mid_low).astype(jnp.bfloat16)
    early = jnp.concatenate([grad_wi, grad_wa, *fold_rows(grad_wo)], 1)
    grad_ctx = contract_cols(grad_mid_low, w_attn).astype(jnp.bfloat16)
    early, grad_ctx = lax.optimization_barrier((early, grad_ctx))
    early = scatter(early)
    grad_qkv = attn_backward(rot, grad_ctx, cos_tab, sin_tab, seg_col, micro, 0, PAIRS)
    grad_h_one = row_major(contract_cols(grad_qkv, w_qkv))
    grad_wq = contract_rows(h_one, grad_qkv).astype(jnp.bfloat16)
    grad_g_one = jnp.sum(grad_h_one * hat_one, 0)
    grad_gains = jnp.stack([grad_g_one, grad_g_two], 1).astype(jnp.bfloat16)
    grad_gains = row_major(jnp.pad(grad_gains, ((0, 0), (0, 126))))
    last = jnp.concatenate([grad_wq, grad_gains], 1)
    early, last = lax.optimization_barrier((early, last))
    last = both_replicas(scatter(last))
    early = both_replicas(early)
    sum_i = early[:, :at_a]
    sum_a = early[:, at_a:at_o]
    sum_o = unfold_rows(early[:, at_o : at_o + width], early[:, at_o + width :])

    sum_q = last[:, : 3 * width]
    sum_g = last[:, 3 * width : 3 * width + 2]
    input_grad = grad_mid + norm_back(grad_h_one, hat_one, inv_one, gain_one)

    qkv_res = adam_update(qkv_weight, qkv_first, qkv_second, sum_q, 0.03)
    attn_res = adam_update(attn_out_weight, attn_first, attn_second, sum_a, 0.3)
    in_res = adam_update(mlp_in_weight, mlp_in_first, mlp_in_second, sum_i, 0.03)
    out_res = adam_update(mlp_out_weight, mlp_out_first, mlp_out_second, sum_o, 0.03)
    gain_res = adam_update(norm_gains, gains_first, gains_second, sum_g, 0.5)
    return (activations, input_grad, *qkv_res, *attn_res, *in_res, *out_res, *gain_res)


def solution(mesh):
    rows_spec = P(("dp", "rep"), None)
    owned = P("dp", None)
    return jax.shard_map(
        functools.partial(local, mesh.shape["rep"]),
        mesh=mesh,
        in_specs=(rows_spec,) * 3 + (owned,) * 15,
        out_specs=(rows_spec,) * 2 + (owned,) * 15,
        check_vma=False,
    )
```
